128 devices in a mesh: ctx: 8 (over z_hi, x), fsdp: 16 (over y, z_lo, core).
Axes of the slice: x: 4, y: 4, z: 4 (z_hi: 2, z_lo: 2; z = z_hi * 2 + z_lo), core: 2. Of those that a mesh axis runs over, the one named last changes fastest.
Arguments:
- inputs: bfloat16 [16, 1024, 1536], P('fsdp', 'ctx'), may hold values from -6 to 6
- block_order: int32 [16], replicated, may hold values from 0 to 15, each once
- routes: int32 [16, 1024, 8], P('fsdp', 'ctx'), may hold values from 0 to 39, all different within a row; in each aligned block of 128 rows (0 to 127, 128 to 255, ..., all dimensions but the last counted through in order) at most 32 rows name the same one
- pre_gain: bfloat16 [1536], P('fsdp'), may hold values from 0.5 to 1.5
- w_query: bfloat16 [1536, 1536], P('fsdp'), may hold values from -0.4375 to 0.4375
- w_key: bfloat16 [1536, 512], P('fsdp'), may hold values from -0.4375 to 0.4375
- w_value: bfloat16 [1536, 512], P('fsdp'), may hold values from -0.15625 to 0.15625
- w_out: bfloat16 [1536, 1536], P('fsdp'), may hold values from -6 to 6
- w_router: bfloat16 [1536, 40], P('fsdp'), may hold values from -0.079589844 to 0.079589844
- mid_gain: bfloat16 [1536], P('fsdp'), may hold values from 0.5 to 1.5
- w_gate: bfloat16 [40, 1536, 512], P('ctx', 'fsdp'), may hold values from -0.15625 to 0.15625
- w_up: bfloat16 [40, 1536, 512], P('ctx', 'fsdp'), may hold values from -0.15625 to 0.15625
- w_down: bfloat16 [40, 512, 1536], P('ctx', 'fsdp'), may hold values from -6 to 6
- cotangent: bfloat16 [16, 1024, 1536], P('fsdp', 'ctx'), may hold values from -6 to 6
Outputs:
- output: bfloat16 [16, 1024, 1536], P('fsdp', 'ctx')
- grad_input: bfloat16 [16, 1024, 1536], P('fsdp', 'ctx')
- grad_pre: float32 [1536], P('fsdp')
- grad_query: float32 [1536, 1536], P('fsdp')
- grad_key: float32 [1536, 512], P('fsdp')
- grad_value: float32 [1536, 512], P('fsdp')
- grad_out: float32 [1536, 1536], P('fsdp')
- grad_router: float32 [1536, 40], P('fsdp')
- grad_mid: float32 [1536], P('fsdp')
- grad_gate: float32 [40, 1536, 512], P('ctx', 'fsdp')
- grad_up: float32 [40, 1536, 512], P('ctx', 'fsdp')
- grad_down: float32 [40, 512, 1536], P('ctx', 'fsdp')
The draws below stay inside these ranges and needn't reach their ends.
Inputs may be any that keep to these rules, and one draw needn't show every extreme that they name: `block_order`: each of 0 to 15 appears once. `routes`: each token names 8 different experts. Among the 128 tokens of one sequence on one device, no expert is named by more than 32 tokens, a bound that some block reaches.
All inputs are finite; a program needn't handle non-finite values.
Results may differ from the reference program's by a relative error of at most 0.028.
Values may be sent and summed in bfloat16 or wider, within the bound.
No kernel may reach another device: no remote copies, remote signals or barrier semaphores. Data moves between devices by JAX's collectives and lax.ppermute only.
A program may use at most 192 MiB of HBM per device.

```python
import math
import jax
import jax.numpy as jnp
import numpy as np
from jax import lax

D = 1536
HEADS = 24
KV_HEADS = 8
HEAD_DIM = 64
FF_E = 512
EXPERTS = 40
TOP = 8
SEQ_LEN = 1024
SEQS = 16
BLOCKS = 16
BLOCK_TOK = 128
MOST = 32
N_CTX = 8


def block_levels(rng, extent, split, low, top_value):
    factor_of = 1.0
    for axis_at, blocks in split:
        heights = jax.random.uniform(jax.random.fold_in(jax.random.fold_in(rng, 6), axis_at), (blocks,), jnp.float32, low / len(split), top_value / len(split))
        factor_of = factor_of * jnp.repeat(jnp.exp(heights), extent[axis_at] // blocks).reshape((-1,) + (1,) * (len(extent) - 1 - axis_at))
    return factor_of


def shared_out(own_key, own, number, rows, amount, top, reach, lean):
    sequence = jax.random.permutation(own_key, amount)
    heavy_load, common = shares(amount, rows * top, reach, lean, True), shares(amount, rows * top, reach, lean, False)
    places = jnp.arange(amount)

    def named(tallies, turn):
        used = int((tallies > 0).sum())
        fixed = max(1, used // 4)
        passed = fixed + (places - fixed + turn * (used - fixed)) % max(1, amount - fixed)
        return jnp.zeros((amount,), jnp.int32).at[sequence[jnp.where(places < fixed, places, passed)]].set(jnp.asarray(tallies, jnp.int32))

    tallies = jnp.where(number % 4 == 0, named(heavy_load, number // 4), named(common, number - number // 4 - 1))
    mixed = jax.random.permutation(jax.random.fold_in(own, 3), amount)
    giver, taker = mixed[0:amount // 2 * 2:2], mixed[1:amount // 2 * 2:2]
    margin = jnp.minimum(tallies[giver] - 1, reach - tallies[taker]) // 2
    margin = jnp.where((giver == sequence[0]) | (taker == sequence[0]) | (tallies[taker] == 0), 0, jnp.maximum(margin, 0))
    passed = jax.random.randint(jax.random.fold_in(own, 4), (amount // 2,), 0, 1 << 20) % (margin + 1)
    tallies = tallies.at[giver].add(-passed).at[taker].add(passed)
    labels = jnp.searchsorted(jnp.cumsum(tallies), jnp.arange(rows * top), side="right").astype(jnp.int32)
    table = labels.reshape(top, rows).T
    table = table[jax.random.permutation(jax.random.fold_in(own, 1), rows)]
    turn = jax.random.randint(jax.random.fold_in(own, 2), (rows, 1), 0, top)
    return jnp.take_along_axis(table, (jnp.arange(top)[None, :] + turn) % top, axis=1)


def shares(amount, total, bound, lean, full):
    weights = [(1 << 20) // math.isqrt(rank ** lean) + 1 for rank in range(1, amount + 1)]
    largest = bound if full else min(bound, max(-(-total // amount), total * weights[0] // sum(weights)))
    least = 1 if total - largest >= amount - 1 else 0
    given, rest = [largest] + [least] * (amount - 1), total - largest - least * (amount - 1)
    while rest > 0:
        movable = [i for i in range(1, amount) if given[i] < largest] or [i for i in range(1, amount) if given[i] < bound]
        whole, budget = sum([weights[i] for i in movable]), rest
        for i in movable:
            extra = min(bound - given[i], max(1, budget * weights[i] // whole), rest)
            given[i] = given[i] + extra
            rest = rest - extra
    return np.array(given)


def gaussian(key, dims, deviation, limit, shards=(), held_as=jnp.bfloat16):
    gain = block_levels(key, dims, shards, -0.22, 0.18) if shards else 1.0
    values = jax.random.normal(key, dims, jnp.float32) * deviation * gain
    return jnp.minimum(jnp.maximum(values, -limit), limit).astype(held_as)


def setup_inputs(seed: int = 0) -> dict:
    key_list = jax.random.split(jax.random.key(seed), 15)
    inputs = gaussian(key_list[0], (SEQS, SEQ_LEN, D), 1.0, 6.0, ((0, 16), (1, 8)))
    block_order = jax.random.permutation(key_list[1], BLOCKS).astype(jnp.int32)
    routes_keys = jax.random.split(jax.random.fold_in(key_list[2], 1), SEQS * SEQ_LEN // BLOCK_TOK)
    routes_turns = jax.random.permutation(jax.random.fold_in(key_list[2], 3), SEQS * SEQ_LEN // BLOCK_TOK)
    routes = jax.vmap(lambda own, number: shared_out(jax.random.fold_in(key_list[2], 2), own, number, BLOCK_TOK, EXPERTS, TOP, MOST, 1))(routes_keys, routes_turns).reshape((SEQS, SEQ_LEN, TOP))
    pre_gain = jnp.clip(1.0 + 0.1 * jax.random.normal(key_list[3], (D,), jnp.float32), 0.5, 1.5).astype(jnp.bfloat16)
    w_query = gaussian(key_list[4], (D, HEADS * HEAD_DIM), (D // 8) ** -0.5, 0.4375, ((0, 16),))
    w_key = gaussian(key_list[5], (D, KV_HEADS * HEAD_DIM), (D // 8) ** -0.5, 0.4375, ((0, 16),))
    w_value = gaussian(key_list[6], (D, KV_HEADS * HEAD_DIM), D ** -0.5, 0.15625, ((0, 16),))
    w_out = gaussian(key_list[7], (HEADS * HEAD_DIM, D), (max(1, HEADS * HEAD_DIM // 1280)) ** -0.5, 6.0, ((0, 16),))
    w_router = gaussian(key_list[8], (D, EXPERTS), 0.0128, 0.079589844, ((0, 16),))
    mid_gain = jnp.clip(1.0 + 0.1 * jax.random.normal(key_list[9], (D,), jnp.float32), 0.5, 1.5).astype(jnp.bfloat16)
    w_gate = gaussian(key_list[10], (EXPERTS, D, FF_E), D ** -0.5, 0.15625, ((0, 8), (1, 16)))
    w_up = gaussian(key_list[11], (EXPERTS, D, FF_E), D ** -0.5, 0.15625, ((0, 8), (1, 16)))
    w_down = gaussian(key_list[12], (EXPERTS, FF_E, D), (max(1, FF_E // 320)) ** -0.5, 6.0, ((0, 8), (1, 16)))
    cotangent = gaussian(key_list[13], (SEQS, SEQ_LEN, D), 1.0, 6.0, ((0, 16), (1, 8)))
    return {"inputs": inputs, "block_order": block_order, "routes": routes, "pre_gain": pre_gain, "w_query": w_query, "w_key": w_key, "w_value": w_value, "w_out": w_out, "w_router": w_router, "mid_gain": mid_gain, "w_gate": w_gate, "w_up": w_up, "w_down": w_down, "cotangent": cotangent}


EPSILON = 1e-06
SCORE_SCALE = 0.015625
RESIDUAL_SCALE = 0.22
THETA_BASE = 10000.0
PRECISE = lax.Precision.HIGHEST

@jax.custom_vjp
def low(v):
    return lax.optimization_barrier(v.astype(jnp.bfloat16)).astype(jnp.float32)

@jax.custom_vjp
def low_back(v):
    return v

def low_keep(v):
    return (low(v), None)

def low_pass(kept, grad):
    return (grad,)

def back_keep(v):
    return (v, None)

def back_low(kept, grad):
    return (low(grad),)
low.defvjp(low_keep, low_pass)
low_back.defvjp(back_keep, back_low)

def rotary_tables(positions):
    half_dim = HEAD_DIM // 2
    freqs = THETA_BASE ** (-2.0 * jnp.arange(half_dim, dtype=jnp.float32) / HEAD_DIM)
    angles = positions.astype(jnp.float32)[:, None] * freqs[None, :]
    cosine_table = jnp.cos(angles)
    sine_table = jnp.sin(angles)
    return (jnp.concatenate([cosine_table, cosine_table], -1), jnp.concatenate([sine_table, sine_table], -1))

def rotate(values, cosine_table, sine_table, turn_sign):
    half_dim = values.shape[-1] // 2
    turned = jnp.concatenate([-values[..., half_dim:], values[..., :half_dim]], -1)
    return values * cosine_table[:, None, :] + turn_sign * turned * sine_table[:, None, :]

def rms_norm(values, gain_vec):
    return values * lax.rsqrt(lax.optimization_barrier(jnp.mean(values * values, axis=-1, keepdims=True)) + EPSILON) * gain_vec

def slots_of(route_rows):
    flat_routes = route_rows.reshape(N_CTX, BLOCK_TOK * TOP)
    onehot = (flat_routes[:, :, None] == jnp.arange(EXPERTS, dtype=jnp.int32)[None, None, :]).astype(jnp.int32)
    ranks = lax.optimization_barrier(jnp.sum(jnp.cumsum(onehot, axis=1) * onehot, axis=2)) - 1
    device_ids = jnp.arange(N_CTX, dtype=jnp.int32)[:, None]
    slot_ids = ((flat_routes * N_CTX + device_ids) * MOST + ranks).reshape(SEQ_LEN * TOP).astype(jnp.int32)
    total_slots = EXPERTS * N_CTX * MOST
    source = jnp.zeros((total_slots,), jnp.int32).at[slot_ids].set(jnp.arange(SEQ_LEN * TOP, dtype=jnp.int32))
    filled = jnp.zeros((total_slots,), jnp.float32).at[slot_ids].set(1.0)
    return (source, filled, slot_ids)

def layer(params, inputs, positions, visible, source, filled, slot_ids, choose):
    pre_gain, w_query, w_key, w_value, w_out, w_router, mid_gain, w_gate, w_up, w_down = params
    head_groups = HEADS // KV_HEADS
    normed1 = low(rms_norm(inputs, pre_gain))
    cosine_table, sine_table = rotary_tables(positions)
    query_raw = low_back(jnp.dot(normed1, w_query, precision=PRECISE))
    query = low(rotate(query_raw.reshape(SEQ_LEN, HEADS, HEAD_DIM), cosine_table, sine_table, 1.0))
    key_raw = low_back(jnp.dot(normed1, w_key, precision=PRECISE))
    keys = low(rotate(key_raw.reshape(SEQ_LEN, KV_HEADS, HEAD_DIM), cosine_table, sine_table, 1.0))
    values = low(low_back(jnp.dot(normed1, w_value, precision=PRECISE))).reshape(SEQ_LEN, KV_HEADS, HEAD_DIM)
    query_split = query.reshape(SEQ_LEN, KV_HEADS, head_groups, HEAD_DIM)
    scores = low_back(jnp.einsum('qjgd,kjd->jgqk', query_split, keys, precision=PRECISE) * SCORE_SCALE)
    probs = low(jax.nn.softmax(jnp.where(visible, scores, -1e+30), axis=-1))
    attended = jnp.einsum('jgqk,kjd->qjgd', probs, values, precision=PRECISE).reshape(SEQ_LEN, HEADS * HEAD_DIM)
    attended = low(low_back(attended))
    mixed = inputs + low_back(RESIDUAL_SCALE * jnp.dot(attended, w_out, precision=PRECISE))
    normed2 = low(rms_norm(mixed, mid_gain))
    logits = jnp.dot(normed2, w_router, precision=PRECISE)
    picked = jnp.einsum('tke,te->tk', choose, logits, precision=PRECISE)
    gates = jax.nn.softmax(picked, axis=-1)
    expert_in = low_back(normed2[source // TOP] * filled[:, None]).reshape(EXPERTS, N_CTX * MOST, D)
    gate_pre = low_back(jnp.einsum('end,edf->enf', expert_in, w_gate, precision=PRECISE))
    up_pre = low_back(jnp.einsum('end,edf->enf', expert_in, w_up, precision=PRECISE))
    hidden = low(jax.nn.silu(gate_pre) * up_pre)
    result = low(low_back(jnp.einsum('enf,efd->end', hidden, w_down, precision=PRECISE)))
    expert_rows = result.reshape(EXPERTS * N_CTX * MOST, D)[slot_ids].reshape(SEQ_LEN, TOP, D)
    return mixed + RESIDUAL_SCALE * lax.optimization_barrier(jnp.sum(gates[:, :, None] * expert_rows, axis=1))

def reference(inputs, block_order, routes, pre_gain, w_query, w_key, w_value, w_out, w_router, mid_gain, w_gate, w_up, w_down, cotangent):
    params = (pre_gain.astype(jnp.float32), w_query.astype(jnp.float32), w_key.astype(jnp.float32), w_value.astype(jnp.float32), w_out.astype(jnp.float32), w_router.astype(jnp.float32), mid_gain.astype(jnp.float32), w_gate.astype(jnp.float32), w_up.astype(jnp.float32), w_down.astype(jnp.float32))
    block_span = SEQ_LEN // (2 * N_CTX)
    offsets = jnp.arange(SEQ_LEN, dtype=jnp.int32)
    positions = (jnp.repeat(block_order, block_span, total_repeat_length=SEQ_LEN) * block_span + offsets % block_span).astype(jnp.int32)
    visible = positions[None, :] <= positions[:, None]

    def one_sequence(totals, items):
        seq_rows, route_rows, grad_rows = items
        source, filled, slot_ids = slots_of(route_rows)
        choose = (route_rows[:, :, None] == jnp.arange(EXPERTS, dtype=jnp.int32)[None, None, :]).astype(jnp.float32)

        def forward(params_in, inputs_in):
            return layer(params_in, inputs_in, positions, visible, source, filled, slot_ids, choose)
        final, pullback = jax.vjp(forward, params, seq_rows.astype(jnp.float32))
        grad_params, grad_in = pullback(grad_rows.astype(jnp.float32))
        totals = jax.tree.map(jnp.add, totals, grad_params)
        return (totals, (final.astype(jnp.bfloat16), grad_in.astype(jnp.bfloat16)))
    zeros = jax.tree.map(jnp.zeros_like, params)
    totals, stacked = lax.scan(one_sequence, zeros, (inputs, routes, cotangent))
    outputs, grad_inputs = stacked
    g_pre, g_query, g_key, g_value, g_out, g_router, g_mid, g_gate, g_up, g_down = totals
    return (outputs, grad_inputs, g_pre, g_query, g_key, g_value, g_out, g_router, g_mid, g_gate, g_up, g_down)
```

```python
import functools
import jax
import jax.numpy as jnp
from jax import lax
from jax.experimental import pallas as pl
from jax.experimental.pallas import tpu as pltpu
from jax.sharding import PartitionSpec as P

D = 1536
HEADS = 24
KV_HEADS = 8
HEAD_DIM = 64
FF = 512
EXPERTS = 40
TOP = 8
SEQ_LEN = 1024
TOK = 128
MOST = 32
N_CTX = 8
LOCAL = EXPERTS // N_CTX
SLOTS = N_CTX * MOST
ROWS = LOCAL * MOST
QW = HEADS * HEAD_DIM // N_CTX
EPSILON = 1e-06
SCORE_SCALE = 0.015625
RES = 0.22
THETA_BASE = 10000.0
BF = jnp.bfloat16
F32 = jnp.float32
MIB = 1 << 20

NT = (((1,), (1,)), ((), ()))
TN = (((0,), (0,)), ((), ()))


def dot(a, b):
    return jnp.dot(a, b, preferred_element_type=F32)


def dotg(a, b, dims):
    return lax.dot_general(a, b, dims, preferred_element_type=F32)


def ctx_pairs(dr, dp):
    return [(z * 4 + x, (z ^ dp) * 4 + (x + dr) % 4) for z in range(2) for x in range(4)]


def fsdp_pairs(dr, dp, dc):
    return [
        (y * 4 + z * 2 + c, ((y + dr) % 4) * 4 + (z ^ dp) * 2 + (c ^ dc))
        for y in range(4)
        for z in range(2)
        for c in range(2)
    ]


def cs(v, dr, dp=0):
    return lax.ppermute(v, "ctx", ctx_pairs(dr, dp))


def fs(v, dr, dp=0, dc=0):
    return lax.ppermute(v, "fsdp", fsdp_pairs(dr, dp, dc))


def gather2(s, send):
    left = send(s, 1)
    right = send(s, -1)
    pair = send(s, 0, 1)
    return [s, right, send(s, 2), left, pair, send(pair, -1), send(pair, 2), send(pair, 1)]


def add_low(a, *rest):
    total = a.astype(F32)
    for r in rest:
        total = total + r.astype(F32)
    return total.astype(BF)


def scatter2_parts(blocks, send):
    b1 = send(blocks[5], 1)
    b2 = send(blocks[6], 2)
    b3 = send(blocks[7], -1)
    a1 = send(blocks[1], 1)
    a2 = send(blocks[2], 2)
    a3 = send(blocks[3], -1)
    p = send(add_low(blocks[4], b1, b2, b3), 0, 1)
    return [blocks[0], a1, a2, a3, p]


def after(v, *done):
    return lax.optimization_barrier((v,) + done)[0]


def halves(v):
    n = v.shape[0] // 2
    return v[:n], v[n:]


def gather3(s, send):
    L = send(s, 1)
    R = send(s, -1)
    Q = send(s, 0, 1)
    L1, L2 = halves(L)
    R1, R2 = halves(R)
    Q1, Q2 = halves(Q)
    A = jnp.concatenate([send(L1, 1), send(R2, -1)])
    QL = jnp.concatenate([send(Q1, 1), send(L2, 0, 1)])
    QR = jnp.concatenate([send(Q1, -1), send(R2, 0, 1)])
    n = s.shape[0] // 3
    QA = jnp.concatenate([send(A[:n], 0, 1), send(QL[n : 2 * n], 1), send(QR[2 * n :], -1)])
    return [s, R, A, L, Q, QR, QA, QL]


def scatter3_first(QA, send):
    n = QA.shape[0] // 3
    return send(QA[:n], 0, 1), send(QA[n : 2 * n], 1), send(QA[2 * n :], -1)


def scatter3_second(A, QR, QL, firsts):
    n = A[0].shape[0] // 3
    g1, g2, g3 = firsts
    cut = lambda v, lo, hi, *more: add_low(v[0][lo:hi], v[1][lo:hi], *more)
    A = jnp.concatenate([cut(A, 0, n, g1), cut(A, n, 3 * n)])
    QR = jnp.concatenate([cut(QR, 0, n), cut(QR, n, 2 * n, g2), cut(QR, 2 * n, 3 * n)])
    QL = jnp.concatenate([cut(QL, 0, 2 * n), cut(QL, 2 * n, 3 * n, g3)])
    return halves(A) + halves(QR) + halves(QL)


def scatter3_send(ops, send):
    A1, A2, R1, R2, L1, L2 = ops
    return (
        send(A1, 1),
        send(R1, 1),
        send(A2, -1),
        send(L1, -1),
        send(R2, 0, 1),
        send(L2, 0, 1),
    )


def scatter3_third(R, L, Q, seconds):
    a1, r1, a2, l1, r2, l2 = seconds
    h, n = a1.shape[0], R[0].shape[0]
    cut = lambda v, lo, hi, *more: add_low(v[0][lo:hi], v[1][lo:hi], *more)
    R = jnp.concatenate([cut(R, 0, h, a1), cut(R, h, n, r2)])
    L = jnp.concatenate([cut(L, 0, h), cut(L, h, n, a2, l2)])
    Q = jnp.concatenate([cut(Q, 0, h, r1, l1), cut(Q, h, n)])
    return R, L, Q


def specs(n):
    return [pl.BlockSpec(memory_space=pltpu.VMEM)] * n


SM = pl.BlockSpec(memory_space=pltpu.SMEM)
HB = pl.BlockSpec(memory_space=pl.ANY)


OUT_BLOCK = pl.BlockSpec((D, D), lambda i: (0, 0))
QKV_BLOCK = pl.BlockSpec((D, 384), lambda i: (0, 4))
X_BLOCK = pl.BlockSpec((TOK, D), lambda i: (0, 0))


def sds(shape, dtype):
    return jax.ShapeDtypeStruct(shape, dtype)


def lane(shape):
    return lax.broadcasted_iota(jnp.int32, shape, 1)


def swap32(v):
    w = v.shape[1]
    up = pltpu.roll(v, w - 32, 1)
    down = pltpu.roll(v, 32, 1)
    return jnp.where(lane(v.shape) % 64 < 32, up, down)


def params(mib=56):
    return pltpu.CompilerParams(vmem_limit_bytes=mib * MIB)


def cost(flops, nbytes):
    return pl.CostEstimate(flops=int(flops), bytes_accessed=int(nbytes), transcendentals=0)


def attn_fwd_kernel(order, *refs):
    xs = refs[:8]
    w, gain, cosb, sinb, posq, posk = refs[8:14]
    h1, qkv, o, lse, kk, vv = refs[14:]
    lo = lane((TOK, 128)) < 64
    for k in range(8):
        b = order[k]
        rows = pl.ds(pl.multiple_of(b * TOK, TOK), TOK)
        x = xs[k][...].astype(F32)
        scaler = lax.rsqrt(jnp.mean(x * x, axis=-1, keepdims=True) + EPSILON)
        h = (x * scaler * gain[...]).astype(BF)
        h1[rows, :] = h
        raw = dot(h, w[...])
        qk = raw[:, :256]
        cos = cosb[rows, :]
        sin = sinb[rows, :]
        cos2 = jnp.concatenate([cos, cos], axis=1)
        sin2 = jnp.concatenate([sin, sin], axis=1)
        rot = qk * cos2 + swap32(qk) * sin2
        t2 = jnp.where(lo, raw[:, 256:], 0.0)
        qkv[rows, :256] = rot.astype(BF)
        qkv[rows, 256:] = t2.astype(BF)
        t1 = rot[:, 128:]
        kk[rows, :] = jnp.where(lo, pltpu.roll(t1, 64, 1), t1).astype(BF)
        vv[rows, :] = (t2 + pltpu.roll(t2, 64, 1)).astype(BF)

    def block(b, carry):
        rows = pl.ds(pl.multiple_of(b * TOK, TOK), TOK)
        vis = posk[...] <= posq[rows, :]
        t0 = qkv[rows, :128]
        t1 = qkv[rows, 128:256]
        zero = jnp.zeros_like(t0)
        outs = []
        logs = []
        for q in (jnp.where(lo, t0, zero), jnp.where(lo, zero, t0), jnp.where(lo, t1, zero)):
            s = dotg(q, kk[...], NT) * SCORE_SCALE
            s = jnp.where(vis, s, -1e30)
            top = jnp.max(s, axis=-1, keepdims=True)
            e = jnp.exp(s - top)
            total = jnp.sum(e, axis=-1, keepdims=True)
            p = (e * (1.0 / total)).astype(BF)
            outs.append(dot(p, vv[...]))
            logs.append(top + jnp.log(total))
        o[b, :, :128] = jnp.where(lo, outs[0], outs[1]).astype(BF)
        o[b, :, 128:] = jnp.where(lo, outs[2], 0.0).astype(BF)
        ln = lane((TOK, 128))
        lse[rows, :] = jnp.where(ln == 0, logs[0], jnp.where(ln == 1, logs[1], logs[2]))
        return carry

    lax.fori_loop(0, 8, block, 0)


def attn_fwd(order, xs, w, gain, cosb, sinb, posq, posk):
    return pl.pallas_call(
        attn_fwd_kernel,
        grid=(1,),
        out_shape=(
            sds((SEQ_LEN, D), BF),
            sds((SEQ_LEN, 384), BF),
            sds((8, TOK, 256), BF),
            sds((SEQ_LEN, 128), F32),
        ),
        in_specs=[SM] + [X_BLOCK] * 8 + [QKV_BLOCK] + specs(5),
        out_specs=tuple(specs(4)),
        scratch_shapes=[pltpu.VMEM((SEQ_LEN, 128), BF), pltpu.VMEM((SEQ_LEN, 128), BF)],
        compiler_params=params(),
        cost_estimate=cost(6e9, 12e6),
        name="attn_fwd",
    )(order, *xs, w, gain, cosb, sinb, posq, posk)


def out_proj_kernel(oa, w_out, x, gain, x2, h2, oc):
    o = jnp.concatenate([oa[s, :, :QW] for s in range(8)], axis=1)
    oc[...] = o
    v = x[...].astype(F32) + RES * dot(o, w_out[...])
    x2[...] = v
    scaler = lax.rsqrt(jnp.mean(v * v, axis=-1, keepdims=True) + EPSILON)
    h2[...] = (v * scaler * gain[...]).astype(BF)


def out_proj(oa, w_out, x, gain):
    return pl.pallas_call(
        out_proj_kernel,
        grid=(1,),
        out_shape=(sds((TOK, D), F32), sds((TOK, D), BF), sds((TOK, D), BF)),
        in_specs=specs(1) + [OUT_BLOCK] + specs(2),
        out_specs=tuple(specs(3)),
        compiler_params=params(),
        cost_estimate=cost(3e9, 8e6),
        name="out_proj",
    )(oa, w_out, x, gain)


def experts_kernel(order, first, *refs):
    h2s = refs[:8]
    xs = refs[8:16]
    wr, pieces, pieces3 = refs[16:19]
    xo, dro, uo, dao, dbo = refs[19:24]
    dhs, yall = refs[24:32], refs[32]
    wg, wu, wd, hbuf, gbuf, rg, dx, pds, gsl = refs[33:42]
    wsem, isem, osem = refs[42:]
    loads = []
    for k in range(8):
        loads.append(pltpu.make_async_copy(h2s[k], hbuf.at[k, :, pl.ds(0, D)], isem.at[0, k]))
        loads.append(pltpu.make_async_copy(xs[k].at[:, pl.ds(D, D + 128)], gbuf.at[k], isem.at[1, k]))
    for c in loads:
        c.start()
    wloads = []
    for k in range(16):
        r96 = pl.ds(k * 96, 96)
        r32 = pl.ds(k * 32, 32)
        for j, (src, dest) in enumerate(
            (
                (pieces.at[k, pl.ds(0, 5)], wg.at[:, r96, :]),
                (pieces.at[k, pl.ds(5, 5)], wu.at[:, r96, :]),
                (pieces3.at[k, pl.ds(10, 5)], wd.at[:, :, r32, :]),
            )
        ):
            wloads.append(pltpu.make_async_copy(src, dest, wsem.at[j, k]))
    for c in wloads:
        c.start()
    start = first[0]
    rowi = lax.broadcasted_iota(jnp.int32, (48, TOK), 0)
    upper = (
        lax.broadcasted_iota(jnp.int32, (TOK, TOK), 0)
        <= lax.broadcasted_iota(jnp.int32, (TOK, TOK), 1)
    ).astype(BF)
    slot = lax.broadcasted_iota(jnp.int32, (MOST, TOK), 0).astype(F32) + 1.0
    for k in range(8):
        loads[2 * k].wait()
        loads[2 * k + 1].wait()
        rt = jnp.transpose(gbuf[k, :, D:].astype(F32)).astype(jnp.int32) - start
        rt = jnp.where(rt < 0, rt + EXPERTS, rt)
        member = rowi == rt[0:1, :]
        for j in range(1, TOP):
            member = member | (rowi == rt[j : j + 1, :])
        mask = jnp.where(member, 1.0, 0.0)
        h = hbuf[k, :, :D]
        logits = jnp.where(member, dotg(wr[...], h, NT), -1e30)
        e = jnp.exp(logits - jnp.max(logits, axis=0, keepdims=True)) * mask
        gates = e / jnp.sum(e, axis=0, keepdims=True)
        rank = dot(mask.astype(BF), upper)
        sel = [
            jnp.where((slot == rank[i : i + 1, :]) & (mask[i : i + 1, :] > 0.0), 1.0, 0.0)
            for i in range(LOCAL)
        ]
        pd = jnp.concatenate(sel, axis=0).astype(BF)
        pds[k] = pd
        xb = dot(pd, h).astype(BF)
        gb = dot(pd, gbuf[k, :, :D]).astype(BF)
        for i in range(LOCAL):
            xo[i, k * MOST : (k + 1) * MOST, :] = xb[i * MOST : (i + 1) * MOST]
            dro[i, k * MOST : (k + 1) * MOST, :] = gb[i * MOST : (i + 1) * MOST]
            gcol = jnp.sum(sel[i] * gates[i : i + 1, :], axis=1, keepdims=True)
            gsl[i, k * MOST : (k + 1) * MOST, :] = jnp.broadcast_to(gcol, (MOST, 128))
    for c in wloads:
        c.wait()

    def expert(i, carry):
        x = xo[i]
        a = dot(x, wg[i])
        b = dot(x, wu[i])
        sig = jax.nn.sigmoid(a)
        act = a * sig
        u = (act * b).astype(BF)
        uo[i] = u
        gcol = gsl[i][:, 0:1]
        at = pl.ds(pl.multiple_of(i * MOST, MOST), MOST)
        du = jnp.zeros((SLOTS, FF), F32)
        dsum = jnp.zeros((SLOTS, 1), F32)
        for j in range(3):
            cols = slice(j * FF, (j + 1) * FF)
            r = dot(u, wd[i, j]).astype(BF).astype(F32)
            gj = dro[i, :, cols].astype(F32)
            dsum = dsum + jnp.sum(r * gj, axis=1, keepdims=True)
            rgj = (r * gcol).astype(BF)
            for k in range(8):
                rg[k, at, cols] = rgj[k * MOST : (k + 1) * MOST]
            drj = ((RES * gcol) * gj).astype(BF)
            dro[i, :, cols] = drj
            du = du + dotg(drj, wd[i, j], NT)
        da = (du * b * sig * (1.0 + a * (1.0 - sig))).astype(BF)
        db = (du * act).astype(BF)
        dao[i] = da
        dbo[i] = db
        dxe = (dotg(da, wg[i], NT) + dotg(db, wu[i], NT)).astype(BF)
        dg = RES * dsum
        hi = dg.astype(BF).astype(F32)
        low = dg - hi
        ln = lane((SLOTS, 128))
        ext = (
            jnp.where(ln == start + i, hi, 0.0) + jnp.where(ln == start + i + 64, low, 0.0)
        ).astype(BF)
        for k in range(8):
            dx[k, at, :D] = dxe[k * MOST : (k + 1) * MOST]
            dx[k, at, D:] = ext[k * MOST : (k + 1) * MOST]
        return carry

    lax.fori_loop(0, LOCAL, expert, 0)
    stores = []
    for k in range(8):
        hbuf[k] = dotg(pds[k], dx[k], TN).astype(BF)
        stores.append(pltpu.make_async_copy(hbuf.at[k], dhs[k], osem.at[0, k]))
        stores[-1].start()
    for k in range(8):
        gbuf[k, :, :D] = dotg(pds[k], rg[k], TN).astype(BF)
        stores.append(
            pltpu.make_async_copy(gbuf.at[k, :, pl.ds(0, D)], yall.at[order[k]], osem.at[1, k])
        )
        stores[-1].start()
    for c in stores:
        c.wait()


def experts(order, first, h2s, xs, wr, pieces):
    return pl.pallas_call(
        experts_kernel,
        out_shape=(
            sds((LOCAL, SLOTS, D), BF),
            sds((LOCAL, SLOTS, D), BF),
            sds((LOCAL, SLOTS, FF), BF),
            sds((LOCAL, SLOTS, FF), BF),
            sds((LOCAL, SLOTS, FF), BF),
        )
        + tuple(sds((TOK, D + 128), BF) for _ in range(8))
        + (sds((8, TOK, D), BF),),
        in_specs=[SM] * 2 + [HB] * 16 + specs(1) + [HB] * 2,
        out_specs=tuple(specs(5) + [HB] * 9),
        scratch_shapes=[
            pltpu.VMEM((LOCAL, D, FF), BF),
            pltpu.VMEM((LOCAL, D, FF), BF),
            pltpu.VMEM((LOCAL, 3, FF, FF), BF),
            pltpu.VMEM((8, TOK, D + 128), BF),
            pltpu.VMEM((8, TOK, D + 128), BF),
            pltpu.VMEM((8, ROWS, D), BF),
            pltpu.VMEM((8, ROWS, D + 128), BF),
            pltpu.VMEM((8, ROWS, TOK), BF),
            pltpu.VMEM((LOCAL, SLOTS, 128), F32),
            pltpu.SemaphoreType.DMA((3, 16)),
            pltpu.SemaphoreType.DMA((2, 8)),
            pltpu.SemaphoreType.DMA((2, 8)),
        ],
        compiler_params=params(60),
        cost_estimate=cost(24e9, 60e6),
        name="experts",
    )(order, first, *h2s, *xs, wr, pieces, pieces.reshape(16, 15, 3, 32, FF))


def expert_grads_kernel(fidx, x, dr, u, da, db, *refs):
    outs, scr, scr2 = refs[:2], refs[2], refs[3]
    xt = x[0]
    for m, d in ((0, da), (1, db)):
        scr[...] = dotg(xt, d[0], TN).astype(BF)
        for k in range(16):
            outs[k // 8][k % 8, m, 0] = scr[pl.ds(pl.multiple_of(fidx[k] * 96, 32), 96), :]
    scr2[...] = dotg(u[0], dr[0], TN).astype(BF)
    for k in range(16):
        at = pl.ds(pl.multiple_of(fidx[k] * 32, 32), 32)
        for j in range(3):
            outs[k // 8][k % 8, 2, 0, j * 32 : (j + 1) * 32, :] = scr2[at, j * FF : (j + 1) * FF]


def expert_grads(fidx, x, dr, u, da, db):
    row = lambda i: (i, 0, 0)
    return pl.pallas_call(
        expert_grads_kernel,
        grid=(LOCAL,),
        out_shape=tuple(sds((8, 3, LOCAL, 96, FF), BF) for _ in range(2)),
        in_specs=[
            SM,
            pl.BlockSpec((1, SLOTS, D), row),
            pl.BlockSpec((1, SLOTS, D), row),
            pl.BlockSpec((1, SLOTS, FF), row),
            pl.BlockSpec((1, SLOTS, FF), row),
            pl.BlockSpec((1, SLOTS, FF), row),
        ],
        out_specs=tuple(
            pl.BlockSpec((8, 3, 1, 96, FF), lambda i: (0, 0, i, 0, 0)) for _ in range(2)
        ),
        scratch_shapes=[pltpu.VMEM((D, FF), BF), pltpu.VMEM((FF, D), BF)],
        compiler_params=params(),
        cost_estimate=cost(8e9, 40e6),
        name="expert_grads",
    )(fidx, x, dr, u, da, db)


def home_kernel(*refs):
    parts = refs[:5]
    x2, h2, gain, g, routes, wr, w_out = refs[5:12]
    dx2o, dod, grouter, gmid = refs[12:]
    total = parts[0][...].astype(F32)
    for p in parts[1:]:
        total = total + p[...].astype(F32)
    ext = total[:, D:]
    ln = lane((TOK, 128))
    dg = jnp.where(ln < EXPERTS, ext + pltpu.roll(ext, 64, 1), 0.0)
    member = ln == routes[:, 0:1]
    for j in range(1, TOP):
        member = member | (ln == routes[:, j : j + 1])
    logits = jnp.where(member, dot(h2[...], wr[...]), -1e30)
    e = jnp.where(member, jnp.exp(logits - jnp.max(logits, axis=1, keepdims=True)), 0.0)
    gates = e / jnp.sum(e, axis=1, keepdims=True)
    dl = gates * (dg - jnp.sum(gates * dg, axis=1, keepdims=True))
    hi = dl.astype(BF)
    low = (dl - hi.astype(F32)).astype(BF)
    dh = total[:, :D] + dotg(hi, wr[...], NT) + dotg(low, wr[...], NT)
    grouter[...] = dotg(h2[...], hi, TN) + dotg(h2[...], low, TN)
    v = x2[...]
    scaler = lax.rsqrt(jnp.mean(v * v, axis=-1, keepdims=True) + EPSILON)
    n = v * scaler
    gmid[...] = jnp.sum(dh * n, axis=0, keepdims=True)
    inner = dh * gain[...]
    dx2 = g[...].astype(F32) + scaler * (inner - n * jnp.mean(inner * n, axis=-1, keepdims=True))
    dx2o[...] = dx2
    dao = dx2.astype(BF)
    pad = jnp.zeros((TOK, 256 - QW), BF)
    for s in range(8):
        do = (RES * dotg(dao, w_out[s * QW : (s + 1) * QW, :], NT)).astype(BF)
        dod[s] = jnp.concatenate([do, pad, dao[:, s * QW : (s + 1) * QW], pad], axis=1)


def home(parts, x2, h2, gain, g, routes, wr, w_out):
    return pl.pallas_call(
        home_kernel,
        grid=(1,),
        out_shape=(
            sds((TOK, D), F32),
            sds((8, TOK, 512), BF),
            sds((D, 128), F32),
            sds((1, D), F32),
        ),
        in_specs=specs(11) + [OUT_BLOCK],
        out_specs=tuple(specs(4)),
        compiler_params=params(),
        cost_estimate=cost(3e9, 10e6),
        name="home_bwd",
    )(*parts, x2, h2, gain, g, routes, wr, w_out)


def attn_bwd_kernel(order, *refs):
    xs = refs[:8]
    qkv, lse, dod, w, cosb, sinb, posq, posk = refs[8:16]
    dhs = refs[16:24]
    dqkv, gpre, kk, vv, dkt, dvt = refs[24:]
    lo = lane((TOK, 128)) < 64
    for b in range(8):
        rows = slice(b * TOK, (b + 1) * TOK)
        t1 = qkv[rows, 128:256].astype(F32)
        t2 = qkv[rows, 256:].astype(F32)
        kk[rows, :] = jnp.where(lo, pltpu.roll(t1, 64, 1), t1).astype(BF)
        vv[rows, :] = (t2 + pltpu.roll(t2, 64, 1)).astype(BF)
    dkt[...] = jnp.zeros_like(dkt)
    dvt[...] = jnp.zeros_like(dvt)

    def block(b, carry):
        rows = pl.ds(pl.multiple_of(b * TOK, TOK), TOK)
        vis = posk[...] <= posq[rows, :]
        t0 = qkv[rows, :128]
        t1 = qkv[rows, 128:256]
        d0 = dod[b, :, :128]
        d1 = dod[b, :, 128:256]
        zero = jnp.zeros_like(t0)
        sides = (
            (jnp.where(lo, t0, zero), jnp.where(lo, d0, zero)),
            (jnp.where(lo, zero, t0), jnp.where(lo, zero, d0)),
            (jnp.where(lo, t1, zero), jnp.where(lo, d1, zero)),
        )
        dqs = []
        dkacc = jnp.zeros((128, SEQ_LEN), F32)
        dvacc = jnp.zeros((128, SEQ_LEN), F32)
        for h, (q, do) in enumerate(sides):
            s = dotg(q, kk[...], NT) * SCORE_SCALE
            p = jnp.where(vis, jnp.exp(s - lse[rows, h : h + 1]), 0.0)
            dp = dotg(do, vv[...], NT)
            delta = jnp.sum(p * dp, axis=-1, keepdims=True)
            ds = (p * (dp - delta)).astype(BF)
            pb = p.astype(BF)
            dqs.append(dot(ds, kk[...]))
            dkacc = dkacc + dotg(q, ds, TN)
            dvacc = dvacc + dotg(do, pb, TN)
        dkt[...] += dkacc
        dvt[...] += dvacc
        dq0 = jnp.where(lo, dqs[0], dqs[1]) * SCORE_SCALE
        dq1 = dqs[2] * SCORE_SCALE
        cos = cosb[rows, :]
        sin = sinb[rows, :]
        dqkv[rows, :128] = (dq0 * cos - swap32(dq0) * sin).astype(BF)
        dqkv[rows, 128:256] = jnp.where(lo, dq1 * cos - swap32(dq1) * sin, 0.0).astype(BF)
        return carry

    lax.fori_loop(0, 8, block, 0)
    dk = jnp.transpose(dkt[...]) * SCORE_SCALE
    dv = jnp.transpose(dvt[...])
    low = lane((SEQ_LEN, 128)) < 64
    dk = dk + pltpu.roll(dk, 64, 1)
    dv = dv + pltpu.roll(dv, 64, 1)
    dk = dk * cosb[...] - swap32(dk) * sinb[...]
    dqkv[:, 128:256] = jnp.where(low, dqkv[:, 128:256].astype(F32), dk).astype(BF)
    dqkv[:, 256:] = jnp.where(low, dv, 0.0).astype(BF)
    acc = jnp.zeros((1, D), F32)
    for k in range(8):
        rows = pl.ds(pl.multiple_of(order[k] * TOK, TOK), TOK)
        dh = dotg(dqkv[rows, :], w[...], NT)
        dhs[k][...] = dh.astype(BF)
        x = xs[k][...].astype(F32)
        scaler = lax.rsqrt(jnp.mean(x * x, axis=-1, keepdims=True) + EPSILON)
        acc = acc + jnp.sum(dh * (x * scaler), axis=0, keepdims=True)
    gpre[...] = acc


def attn_bwd(order, xs, qkv, lse, dod, w, cosb, sinb, posq, posk):
    return pl.pallas_call(
        attn_bwd_kernel,
        grid=(1,),
        out_shape=tuple(sds((TOK, D), BF) for _ in range(8))
        + (sds((SEQ_LEN, 384), BF), sds((1, D), F32)),
        in_specs=[SM] + [X_BLOCK] * 8 + specs(3) + [QKV_BLOCK] + specs(4),
        out_specs=tuple(specs(10)),
        scratch_shapes=[
            pltpu.VMEM((SEQ_LEN, 128), BF),
            pltpu.VMEM((SEQ_LEN, 128), BF),
            pltpu.VMEM((128, SEQ_LEN), F32),
            pltpu.VMEM((128, SEQ_LEN), F32),
        ],
        compiler_params=params(),
        cost_estimate=cost(12e9, 14e6),
        name="attn_bwd",
    )(order, *xs, qkv, lse, dod, w, cosb, sinb, posq, posk)


def attn_grads_kernel(h1, dqkv, dod, ocs, grouter, gpre, gmid, outs, scr):
    scr[:, :384] = dotg(h1[...], dqkv[...], TN).astype(BF)
    acc = jnp.zeros((D, 256), F32)
    for k in range(8):
        acc = acc + dotg(ocs[k], dod[k, :, 256:], TN)
    scr[:, 384:] = (RES * acc).astype(BF)
    pre = jnp.transpose(jnp.broadcast_to(gpre[...], (128, D)))
    mid = jnp.transpose(jnp.broadcast_to(gmid[...], (128, D)))
    ln = lane((D, 128))
    ext = pltpu.roll(grouter[...], 64, 1)
    ext = jnp.where(ln == 104, pre, jnp.where(ln == 105, mid, ext)).astype(BF)
    scr[:, 256:384] = jnp.where(ln < 64, scr[:, 256:384], ext)
    for k in range(16):
        outs[k] = scr[k * 96 : (k + 1) * 96, :]


def attn_grads(h1, dqkv, dod, ocs, grouter, gpre, gmid):
    return pl.pallas_call(
        attn_grads_kernel,
        out_shape=sds((16, 96, 640), BF),
        in_specs=specs(7),
        out_specs=specs(1)[0],
        scratch_shapes=[pltpu.VMEM((D, 640), BF)],
        compiler_params=params(),
        cost_estimate=cost(4e9, 12e6),
        name="attn_grads",
    )(h1, dqkv, dod, ocs, grouter, gpre, gmid)


def expert_out_kernel(keep, got, a, b, c, gate, up, down):
    for m, out in ((0, gate), (1, up), (2, down)):
        for e in range(LOCAL):
            i = m * LOCAL + e
            v = keep[0, m, e].astype(F32) + got[0, m, e].astype(F32)
            v = v + a[i].astype(F32) + b[i].astype(F32) + c[i].astype(F32)
            if m < 2:
                out[e] = v
            else:
                for j in range(3):
                    out[e, :, j * FF : (j + 1) * FF] = v[j * 32 : (j + 1) * 32]


def expert_out(keep, got, parts):
    mine = pl.BlockSpec((1, 3, LOCAL, 96, FF), lambda i: (0, 0, 0, 0, 0))
    return pl.pallas_call(
        expert_out_kernel,
        grid=(1,),
        out_shape=(
            sds((LOCAL, 96, FF), F32),
            sds((LOCAL, 96, FF), F32),
            sds((LOCAL, 32, D), F32),
        ),
        in_specs=[mine, mine] + specs(3),
        out_specs=tuple(specs(3)),
        compiler_params=params(),
        cost_estimate=cost(1e6, 10e6),
        name="expert_out",
    )(keep, got, *parts)


def attn_out_kernel(full, gq, gk, gv, go, ext):
    pick = lambda lo, hi: jnp.concatenate([full[c, :, lo:hi] for c in range(8)], axis=1)
    gq[...] = pick(0, QW).astype(F32)
    gk[...] = pick(QW, QW + 64).astype(F32)
    gv[...] = pick(QW + 64, QW + 128).astype(F32)
    go[...] = pick(384, 384 + QW).astype(F32)
    total = full[0, :, 256:384].astype(F32)
    for c in range(1, 8):
        total = total + full[c, :, 256:384].astype(F32)
    ext[...] = pltpu.roll(total, 64, 1)


def attn_out(full):
    return pl.pallas_call(
        attn_out_kernel,
        out_shape=(
            sds((96, D), F32),
            sds((96, 512), F32),
            sds((96, 512), F32),
            sds((96, D), F32),
            sds((96, 128), F32),
        ),
        in_specs=specs(1),
        out_specs=tuple(specs(5)),
        compiler_params=params(),
        cost_estimate=cost(1e6, 3e6),
        name="attn_out",
    )(full)


def input_grad_kernel(*refs):
    parts = refs[:5]
    x, dx2, gain, out = refs[5:]
    dh = parts[0][...].astype(F32)
    for p in parts[1:]:
        dh = dh + p[...].astype(F32)
    v = x[...].astype(F32)
    scaler = lax.rsqrt(jnp.mean(v * v, axis=-1, keepdims=True) + EPSILON)
    n = v * scaler
    inner = dh * gain[...]
    dx1 = scaler * (inner - n * jnp.mean(inner * n, axis=-1, keepdims=True))
    out[...] = (dx2[...] + dx1).astype(BF)


def input_grad(parts, x, dx2, gain):
    return pl.pallas_call(
        input_grad_kernel,
        out_shape=sds((TOK, D), BF),
        in_specs=specs(8),
        out_specs=specs(1)[0],
        compiler_params=params(),
        cost_estimate=cost(1e6, 4e6),
        name="input_grad",
    )(*parts, x, dx2, gain)


def on_device(
    inputs,
    block_order,
    routes,
    pre_gain,
    w_query,
    w_key,
    w_value,
    w_out,
    w_router,
    mid_gain,
    w_gate,
    w_up,
    w_down,
    cotangent,
):
    ci = lax.axis_index("ctx")
    fi = lax.axis_index("fsdp")
    kr = jnp.arange(8, dtype=jnp.int32)
    order = ((ci // 4) ^ (kr // 4)) * 4 + (ci % 4 + kr % 4) % 4
    chips = ((fi // 4 + kr % 4) % 4) * 4 + (((fi // 2) % 2) ^ (kr // 4)) * 2
    fidx = jnp.concatenate([chips + fi % 2, chips + (1 - fi % 2)]).astype(jnp.int32)
    first = (ci * LOCAL).reshape(1).astype(jnp.int32)
    order = order.astype(jnp.int32)

    x = inputs[0]
    g = cotangent[0]
    xg = jnp.concatenate([x, g, routes[0].astype(BF), jnp.zeros((TOK, 120), BF)], axis=1)
    xs = gather2(xg, cs)

    q_c = lax.dynamic_slice_in_dim(w_query, ci * QW, QW, 1)
    k_c = lax.dynamic_slice_in_dim(w_key, ci * 64, 64, 1)
    v_c = lax.dynamic_slice_in_dim(w_value, ci * 64, 64, 1)
    pack = jnp.concatenate(
        [w_out, q_c, k_c, v_c, w_router, pre_gain[:, None], mid_gain[:, None], jnp.zeros((96, 22), BF)],
        axis=1,
    )
    weights = lax.all_gather(pack, "fsdp", axis=0, tiled=True)
    weights = after(weights, *xs)
    pre_row = weights[:, 1896:1897].reshape(1, D).astype(F32)
    mid_row = weights[:, 1897:1898].reshape(1, D).astype(F32)
    wr = weights[:, 1856:1896]
    wr_pad = jnp.pad(wr, ((0, 0), (0, 88)))
    wr_t = jnp.pad(jnp.roll(jnp.transpose(wr), -ci * LOCAL, axis=0), ((0, 8), (0, 0)))

    down3 = w_down.reshape(LOCAL, 32, 3, FF).transpose(0, 2, 1, 3).reshape(LOCAL, 96, FF)
    shard = jnp.concatenate([w_gate, w_up, down3], axis=0)
    pieces = lax.all_gather(shard, "fsdp", axis=0, tiled=False)

    span = SEQ_LEN // block_order.shape[0]
    pos = (block_order[:, None] * span + jnp.arange(span, dtype=jnp.int32)[None, :]).reshape(SEQ_LEN)
    freqs = THETA_BASE ** (-2.0 * jnp.arange(32, dtype=F32) / HEAD_DIM)
    angles = pos.astype(F32)[:, None] * freqs[None, :]
    cos = jnp.cos(angles)
    sin = jnp.sin(angles)
    cosb = jnp.concatenate([cos, cos, cos, cos], axis=1)
    sinb = jnp.concatenate([-sin, sin, -sin, sin], axis=1)
    posq = pos[:, None]
    posk = pos[None, :]

    h1, qkv, o, lse = attn_fwd(order, xs, weights, pre_row, cosb, sinb, posq, posk)
    oa = lax.all_to_all(o, "ctx", 0, 0, tiled=True)
    x2, h2, oc = out_proj(oa, weights, x, mid_row)
    h2s = gather2(h2, cs)
    ocb = jnp.broadcast_to(after(oc, *h2s), (8, TOK, D))
    ocs = lax.all_to_all(ocb, "ctx", 0, 0, tiled=True)
    outs = experts(order, first, h2s, xs, wr_t, pieces)
    xe, dre, ue, dae, dbe = outs[:5]
    dhs, yall = list(outs[5:13]), outs[13]
    parts = scatter2_parts(dhs, cs)
    keep, give = expert_grads(fidx, after(xe, ocs), dre, ue, dae, dbe)
    got = fs(give, 0, 0, 1)

    def chips(*done):
        kept, swapped = lax.optimization_barrier((keep, got) + done)[:2]
        kept = kept.reshape(8, 15, 96, FF)
        swapped = swapped.reshape(8, 15, 96, FF)
        return lambda k: (kept[k], swapped[k])

    e1 = scatter3_first(add_low(*chips()(6)), fs)
    dx2, dod, grouter, gmid = home(
        parts, x2, h2, after(mid_row, got), g, routes[0], wr_pad, weights
    )
    dod = lax.all_to_all(dod, "ctx", 0, 0, tiled=True)
    chip = chips(*e1)
    e2 = scatter3_second(chip(2), chip(5), chip(7), e1)
    dod = after(dod, *e2)
    chip = chips(*e2)
    e2 = scatter3_send(e2, fs)
    yg = lax.all_to_all(after(yall, dod), "ctx", 0, 0, tiled=True)
    ab = attn_bwd(order, xs, qkv, lse, dod, weights, cosb, sinb, posq, posk)
    dh1s, dqkv, gpre = ab[:8], ab[8], ab[9]
    p1 = scatter2_parts(dh1s, cs)
    e3 = scatter3_third(chip(1), chip(3), chip(4), e2)
    ag = attn_grads(h1, dqkv, dod, ocs, grouter, gpre, after(gmid, *e3))
    e3 = (fs(e3[0], 1), fs(e3[1], -1), fs(e3[2], 0, 1))
    ag = lax.all_to_all(after(ag, yg), "fsdp", 0, 0, tiled=True)
    ag = after(ag, *p1[1:], *e3)
    ashard = jnp.sum(ag.astype(F32), axis=0).astype(BF)
    ashard = jnp.broadcast_to(ashard, (8, 96, 640))
    full = lax.all_to_all(ashard, "ctx", 0, 0, tiled=True)
    gq, gk, gv, go, ext = attn_out(full)
    gate, up, down = expert_out(keep, got, e3)

    output = (x2 + RES * jnp.sum(yg.astype(F32), axis=0)).astype(BF)[None]
    grad_input = input_grad(p1, x, dx2, pre_row)[None]
    return (
        output,
        grad_input,
        ext[:, 40],
        gq,
        gk,
        gv,
        go,
        ext[:, :40],
        ext[:, 41],
        gate,
        up,
        down,
    )


def solution(mesh):
    return jax.shard_map(
        on_device,
        mesh=mesh,
        in_specs=(
            P("fsdp", "ctx", None),
            P(),
            P("fsdp", "ctx", None),
            P("fsdp"),
            P("fsdp", None),
            P("fsdp", None),
            P("fsdp", None),
            P("fsdp", None),
            P("fsdp", None),
            P("fsdp"),
            P("ctx", "fsdp", None),
            P("ctx", "fsdp", None),
            P("ctx", "fsdp", None),
            P("fsdp", "ctx", None),
        ),
        out_specs=(
            P("fsdp", "ctx", None),
            P("fsdp", "ctx", None),
            P("fsdp"),
            P("fsdp", None),
            P("fsdp", None),
            P("fsdp", None),
            P("fsdp", None),
            P("fsdp", None),
            P("fsdp"),
            P("ctx", "fsdp", None),
            P("ctx", "fsdp", None),
            P("ctx", "fsdp", None),
        ),
        check_vma=False,
    )
```
